32 devices in a mesh: seq: 8 (over z, y), head: 4 (over x, core).
Axes of the slice: x: 2, y: 2, z: 4, core: 2. Of those that a mesh axis runs over, the one named last changes fastest.
Arguments:
- queries: bfloat16 [4096, 4096], P('seq', 'head'), may hold values from -8 to 8
- keys: bfloat16 [4096, 4096], P('seq', 'head'), may hold values from -8 to 8
- values: bfloat16 [4096, 4096], P('seq', 'head'), may hold values from -6 to 6
- w_out: bfloat16 [4096, 4096], P('head', 'seq'), may hold values from -0.125 to 0.125
- grad_y: bfloat16 [4096, 4096], P('seq', 'head'), may hold values from -6 to 6
Outputs:
- mixer_result: bfloat16 [4096, 4096], P('seq', 'head')
- grad_queries: bfloat16 [4096, 4096], P('seq', 'head')
- grad_keys: bfloat16 [4096, 4096], P('seq', 'head')
- grad_values: bfloat16 [4096, 4096], P('seq', 'head')
- projection_sensitivity: float32 [4096, 4096], P('head', 'seq')
The draws below stay inside these ranges and needn't reach their ends.
All inputs are finite; a program needn't handle non-finite values.
Results may differ from the reference program's by a relative error of at most 0.025.
Values may be sent and summed in bfloat16 or wider, within the bound.
A program may use at most 128 MiB of HBM per device.

```python
import math
import jax
import jax.numpy as jnp
from jax import lax

H = 32
DH = 128
D = 4096
BLOCK = 64
BAND = 8
TOK_DEV = 512
TOKENS = 4096
N_SEQ = 8
N_HEAD = 4


def pair_rows(key):
    base = jax.random.fold_in(key, 11)
    key_q, key_k = jax.random.split(base, 2)
    query = jnp.clip(jax.random.normal(key_q, (TOKENS, D), jnp.float32), -6.0, 6.0)
    keyed = jnp.clip(jax.random.normal(key_k, (TOKENS, D), jnp.float32), -6.0, 6.0)
    return (query, keyed)


def draw_queries(key, part):
    return pair_rows(key)[0].astype(jnp.bfloat16)


def draw_keys(key, part):
    return pair_rows(key)[1].astype(jnp.bfloat16)


def with_spikes(drawn, own_key, source, target, shards_of, factor):
    def block_of(dim):
        return (jnp.arange(drawn.shape[dim]) // (drawn.shape[dim] // shards_of)).reshape((-1,) + (1,) * (drawn.ndim - 1 - dim))

    one_side = jax.random.permutation(own_key, shards_of)[block_of(target)]
    far = (block_of(target) + shards_of // 2) % shards_of
    return jnp.where((block_of(source) == one_side) | (block_of(source) == far), factor * drawn, drawn)


def steps_of(rng, dims, cuts, low, largest):
    factor_of, own = 1.0, jax.random.fold_in(rng, 6)
    for position, blocks in cuts:
        heights = jnp.exp(jax.random.uniform(jax.random.fold_in(own, position), (blocks,), jnp.float32, low / len(cuts), largest / len(cuts)))
        factor_of = factor_of * jnp.repeat(heights, dims[position] // blocks).reshape([-1 if axis == position else 1 for axis in range(len(dims))])
    return factor_of


def noise(stream_key, shape, scale, bound, pieces=(), kind=jnp.bfloat16):
    values = jax.random.normal(stream_key, shape, jnp.float32) * scale
    if len(pieces) > 0:
        values = steps_of(stream_key, shape, pieces, -0.22, 0.18) * values
    return jnp.clip(values, min=-bound, max=bound).astype(kind)


def gaussian_with(rng, dims, spread, limit, shards, heavy, kind=jnp.bfloat16):
    entries = spread * jax.random.normal(rng, dims, jnp.float32)
    if shards:
        entries = entries * steps_of(rng, dims, shards, -0.22, 0.18)
    return jnp.clip(with_spikes(entries, jax.random.fold_in(rng, 3), *heavy), -limit, limit).astype(kind)


def setup_inputs(seed: int = 0) -> dict:
    arg_keys = jax.random.split(jax.random.key(seed), 6)
    return {
        "queries": draw_queries(jax.random.fold_in(arg_keys[5], 71), 0),
        "keys": draw_keys(jax.random.fold_in(arg_keys[5], 71), 0),
        "values": noise(arg_keys[2], (TOKENS, D), 1.0, 6.0, ((0, 8), (1, 4))),
        "w_out": gaussian_with(arg_keys[3], (D, D), D ** -0.5, 0.125, ((0, 4), (1, 8)), (0, 1, 8, 2.0)),
        "grad_y": gaussian_with(arg_keys[4], (TOKENS, D), 1.0, 6.0, ((0, 8), (1, 4)), (0, 1, 8, 2.0)),
    }


EPSILON = 1e-05
MASKED = -1e+30

def band_allowed(first, rows, span):
    query = first + jnp.arange(rows, dtype=jnp.int32)
    place = first - (BAND - 1) * BLOCK + jnp.arange(span, dtype=jnp.int32)
    near = place[:, None] // BLOCK >= query[:, None].T // BLOCK - (BAND - 1)
    return (place[:, None] <= query[None, :]) & near & (place[:, None] >= 0)

def score_of(first, q_rows, k_span):
    rows = q_rows.shape[0]
    span = k_span.shape[0]
    score = jnp.dot(k_span, q_rows.T, preferred_element_type=jnp.float32) * (1.0 / math.sqrt(DH))
    return jnp.where(band_allowed(first, rows, span), score, MASKED)

def linear_forward(q_head, k_head, v_head):
    block_count = q_head.shape[0] // BLOCK
    query_block_rows = q_head.reshape(block_count, BLOCK, DH).astype(jnp.float32)
    lookup_tile_entries = k_head.reshape(block_count, BLOCK, DH).astype(jnp.float32)
    value_block_rows = v_head.reshape(block_count, BLOCK, DH).astype(jnp.float32)
    cross_block_totals = jnp.einsum('mpl,mpw->mlw', lookup_tile_entries, value_block_rows)
    running_state = (jnp.cumsum(cross_block_totals, axis=0) - cross_block_totals).astype(jnp.bfloat16)
    causal = jnp.arange(BLOCK)[:, None] >= jnp.arange(BLOCK)[None, :]
    inside_block_scores = jnp.where(causal, jnp.einsum('ntk,njk->ntj', query_block_rows, lookup_tile_entries), 0.0).astype(jnp.bfloat16)
    linear_branch = jnp.einsum('wqf,wfa->wqa', query_block_rows, running_state.astype(jnp.float32))
    linear_branch = linear_branch + jnp.einsum('ntj,njv->ntv', inside_block_scores.astype(jnp.float32), value_block_rows)
    linear_branch = linear_branch.reshape(-1, DH)
    inv_rms = lax.rsqrt(lax.optimization_barrier(jnp.mean(linear_branch * linear_branch, axis=-1, keepdims=True)) + EPSILON)
    return (running_state, inside_block_scores, linear_branch * inv_rms, inv_rms)

def window_forward(q_head, k_head, v_head):
    rows = BAND * BLOCK
    edge = (BAND - 1) * BLOCK
    span = rows + edge
    length = q_head.shape[0]
    k_wide = jnp.concatenate([jnp.zeros((edge, DH), k_head.dtype), k_head])
    v_wide = jnp.concatenate([jnp.zeros((edge, DH), v_head.dtype), v_head])

    def one_block(index):
        first = index * rows
        q_rows = lax.dynamic_slice_in_dim(q_head, first, rows, 0)
        k_span = lax.dynamic_slice_in_dim(k_wide, first, span, 0)
        v_span = lax.dynamic_slice_in_dim(v_wide, first, span, 0)
        score = score_of(first, q_rows, k_span)
        row_max = lax.optimization_barrier(jnp.max(score, axis=0))
        raised = jnp.exp(score - row_max[None, :])
        inv_total = 1.0 / lax.optimization_barrier(jnp.sum(raised, axis=0))
        probs = (raised * inv_total[None, :]).astype(jnp.bfloat16)
        return (jnp.dot(probs.T, v_span, preferred_element_type=jnp.float32), row_max, inv_total)
    outs, row_max, inv_total = lax.map(one_block, jnp.arange(length // rows, dtype=jnp.int32))
    return (outs.reshape(length, DH), row_max, inv_total, k_wide, v_wide)

def head_mixed(parts):
    q_head, k_head, v_head = parts
    running_state, inside_block_scores, normed, inv_rms = linear_forward(q_head, k_head, v_head)
    window, row_max, inv_total, k_wide, v_wide = window_forward(q_head, k_head, v_head)
    return (normed + window).astype(jnp.bfloat16)

def head_backward(parts):
    q_head, k_head, v_head, grad_head = parts
    length = q_head.shape[0]
    rows = BAND * BLOCK
    edge = (BAND - 1) * BLOCK
    span = rows + edge
    score_scale = 1.0 / math.sqrt(DH)
    running_state, inside_block_scores, normed, inv_rms = linear_forward(q_head, k_head, v_head)
    window, row_max, inv_total, k_wide, v_wide = window_forward(q_head, k_head, v_head)
    grad_f = grad_head.astype(jnp.float32)
    delta = lax.optimization_barrier(jnp.sum(grad_f * window, axis=-1))
    inner = lax.optimization_barrier(jnp.mean(grad_f * normed, axis=-1, keepdims=True))
    grad_lin = (inv_rms * (grad_f - normed * inner)).astype(jnp.bfloat16)
    block_count = length // BLOCK
    query_block_rows = q_head.reshape(block_count, BLOCK, DH).astype(jnp.float32)
    lookup_tile_entries = k_head.reshape(block_count, BLOCK, DH).astype(jnp.float32)
    value_block_rows = v_head.reshape(block_count, BLOCK, DH).astype(jnp.float32)
    upstream_tile_entries = grad_lin.reshape(block_count, BLOCK, DH).astype(jnp.float32)
    reverse_state_totals = jnp.einsum('xlm,xla->xma', query_block_rows, upstream_tile_entries)
    back_state = (lax.optimization_barrier(jnp.sum(reverse_state_totals, axis=0))[None] - jnp.cumsum(reverse_state_totals, axis=0)).astype(jnp.bfloat16)
    causal = jnp.arange(BLOCK)[:, None] >= jnp.arange(BLOCK)[None, :]
    intra_grad = jnp.where(causal, jnp.einsum('ntv,njv->ntj', upstream_tile_entries, value_block_rows), 0.0).astype(jnp.bfloat16)
    cumulative_memory_single = running_state.astype(jnp.float32)
    reverse_state_float = back_state.astype(jnp.float32)
    local_derivative_single = intra_grad.astype(jnp.float32)
    asking_plain_entries = jnp.einsum('nrq,nhq->nrh', upstream_tile_entries, cumulative_memory_single) + jnp.einsum('wri,wid->wrd', local_derivative_single, lookup_tile_entries)
    key_linear_rows = jnp.einsum('lou,leu->loe', value_block_rows, reverse_state_float) + jnp.einsum('uda,udr->uar', local_derivative_single, query_block_rows)
    value_linear_rows = jnp.einsum('uwb,ubc->uwc', lookup_tile_entries, reverse_state_float) + jnp.einsum('owu,owh->ouh', inside_block_scores.astype(jnp.float32), upstream_tile_entries)

    def one_back(index, carry):
        q_acc, k_acc, v_acc = carry
        first = (index * rows).astype(jnp.int32)
        q_rows = lax.dynamic_slice_in_dim(q_head, first, rows, 0)
        k_span = lax.dynamic_slice_in_dim(k_wide, first, span, 0)
        v_span = lax.dynamic_slice_in_dim(v_wide, first, span, 0)
        grad_rows = lax.dynamic_slice_in_dim(grad_head, first, rows, 0)
        score = score_of(first, q_rows, k_span)
        probs = (jnp.exp(score - row_max[index][None, :]) * inv_total[index][None, :]).astype(jnp.bfloat16)
        dprob = jnp.dot(v_span, grad_rows.T, preferred_element_type=jnp.float32)
        delta_rows = lax.dynamic_slice_in_dim(delta, first, rows, 0)
        dscore = (probs.astype(jnp.float32) * (dprob - delta_rows[None, :]) * score_scale).astype(jnp.bfloat16)
        q_acc = lax.dynamic_update_slice_in_dim(q_acc, jnp.dot(dscore.T, k_span, preferred_element_type=jnp.float32), first, 0)
        k_new = lax.dynamic_slice_in_dim(k_acc, first, span, 0) + jnp.dot(dscore, q_rows, preferred_element_type=jnp.float32)
        v_new = lax.dynamic_slice_in_dim(v_acc, first, span, 0) + jnp.dot(probs, grad_rows, preferred_element_type=jnp.float32)
        k_acc = lax.dynamic_update_slice_in_dim(k_acc, k_new, first, 0)
        v_acc = lax.dynamic_update_slice_in_dim(v_acc, v_new, first, 0)
        return (q_acc, k_acc, v_acc)
    start_carry = (jnp.zeros((length, DH), jnp.float32), jnp.zeros((length + edge, DH), jnp.float32), jnp.zeros((length + edge, DH), jnp.float32))
    q_window, k_window, v_window = lax.fori_loop(0, length // rows, one_back, start_carry)
    grad_q = (asking_plain_entries.reshape(length, DH) + q_window).astype(jnp.bfloat16)
    grad_k = (key_linear_rows.reshape(length, DH) + k_window[edge:]).astype(jnp.bfloat16)
    grad_v = (value_linear_rows.reshape(length, DH) + v_window[edge:]).astype(jnp.bfloat16)
    return (grad_q, grad_k, grad_v)

def reference(queries, keys, values, w_out, grad_y):
    length = queries.shape[0]

    def by_head(array):
        return array.reshape(length, H, DH).transpose(1, 0, 2)

    def by_token(array):
        return array.transpose(1, 0, 2).reshape(length, D)
    heads = (by_head(queries), by_head(keys), by_head(values))
    mixed = by_token(lax.map(head_mixed, heads))
    group_width = H // N_HEAD * DH
    layer_total = jnp.zeros((length, D), jnp.float32)
    for group in range(N_HEAD):
        low = group * group_width
        part_sum = jnp.dot(mixed[:, low:low + group_width], w_out[low:low + group_width], preferred_element_type=jnp.float32).astype(jnp.bfloat16)
        layer_total = layer_total + lax.optimization_barrier(part_sum).astype(jnp.float32)
    mixer_result = layer_total.astype(jnp.bfloat16)
    grad_mixed = lax.dot_general(grad_y, w_out, (((1,), (1,)), ((), ())), preferred_element_type=jnp.float32).astype(jnp.bfloat16)

    def add_run(index, total):
        first = (index * TOK_DEV).astype(jnp.int32)
        mixed_run = lax.dynamic_slice_in_dim(mixed, first, TOK_DEV, 0)
        grad_run = lax.dynamic_slice_in_dim(grad_y, first, TOK_DEV, 0)
        term = lax.dot_general(mixed_run, grad_run, (((0,), (0,)), ((), ())), preferred_element_type=jnp.float32).astype(jnp.bfloat16)
        return total + lax.optimization_barrier(term).astype(jnp.float32)
    grad_total = lax.fori_loop(0, N_SEQ, add_run, jnp.zeros((D, D), jnp.float32))
    projection_sensitivity = grad_total * TOKENS ** (-0.5)
    grad_q, grad_k, grad_v = lax.map(head_backward, heads + (by_head(grad_mixed),))
    return (mixer_result, by_token(grad_q), by_token(grad_k), by_token(grad_v), projection_sensitivity)
```

```python
import math

import jax
import jax.numpy as jnp
from jax import lax
from jax.experimental import pallas as pl
from jax.experimental.pallas import tpu as pltpu
from jax.sharding import PartitionSpec as P

DH = 128
BLOCK = 64
BAND = 8
TILE = 128
EDGE = (BAND - 1) * BLOCK
LEAD = BAND * BLOCK
SPAN = LEAD + TILE
EPSILON = 1e-05
MASKED = -1e30
SCALE = 1.0 / math.sqrt(DH)
LOG2E = 1.0 / math.log(2.0)
F32 = jnp.float32
BF16 = jnp.bfloat16


def mm(a, b):
    return jnp.dot(a, b, preferred_element_type=F32)


def mm_nt(a, b):
    return lax.dot_general(a, b, (((1,), (1,)), ((), ())), preferred_element_type=F32)


def widen(wide, edge_ref, own_ref):
    wide[0 : LEAD - EDGE, :] = jnp.zeros((LEAD - EDGE, DH), wide.dtype)
    wide[LEAD - EDGE : LEAD, :] = edge_ref[...]
    wide[LEAD:, :] = own_ref[...]


def causal_t():
    key = lax.broadcasted_iota(jnp.int32, (TILE, TILE), 0)
    query = lax.broadcasted_iota(jnp.int32, (TILE, TILE), 1)
    return key <= query


def forward_kernel(
    first_ref, q_ref, k_ref, v_ref, ke_ref, ve_ref, before_ref,
    mixed_ref, probs_ref, win_ref, norm_ref, inv_ref, state_ref,
    kw, vw,
):
    tiles = q_ref.shape[0] // TILE
    widen(kw, ke_ref, k_ref)
    widen(vw, ve_ref, v_ref)
    vt = vw[...].T
    first = first_ref[0]
    key = lax.broadcasted_iota(jnp.int32, (SPAN, TILE), 0)
    query = lax.broadcasted_iota(jnp.int32, (SPAN, TILE), 1)
    low = (query // BLOCK + 1) * BLOCK
    high = query + LEAD
    causal = causal_t()
    state = before_ref[0]
    for i in range(tiles):
        rows = slice(i * TILE, (i + 1) * TILE)
        q = q_ref[rows, :]
        raw = mm_nt(kw[i * TILE : i * TILE + SPAN, :], q)
        allowed = (key >= jnp.maximum(low, LEAD - i * TILE - first)) & (key <= high)
        score = jnp.where(allowed, raw, MASKED)
        row_max = jnp.max(score, axis=0, keepdims=True)
        raised = jnp.exp2((score - row_max) * (SCALE * LOG2E))
        inv_total = 1.0 / jnp.sum(raised, axis=0, keepdims=True)
        probs = (raised * inv_total).astype(BF16)
        probs_ref[0, i] = probs
        window = mm(vt[:, i * TILE : i * TILE + SPAN], probs)
        vt_own = vt[:, LEAD + i * TILE : LEAD + (i + 1) * TILE]
        intra = jnp.where(causal, raw[LEAD:], 0.0).astype(BF16)
        rounded = state.astype(BF16)
        state_ref[0, i] = rounded
        linear = mm(vt_own, intra) + mm_nt(rounded, q)
        state = state + mm(vt_own, k_ref[rows, :])
        inv = lax.rsqrt(jnp.mean(linear * linear, axis=0, keepdims=True) + EPSILON)
        normed = linear * inv
        win_ref[0, i] = window
        norm_ref[0, i] = normed
        inv_ref[0, i] = inv
        mixed_ref[rows, :] = (normed + window).T.astype(BF16)


def backward_kernel(
    q_ref, k_ref, v_ref, ke_ref, ve_ref, g_ref,
    probs_ref, win_ref, norm_ref, inv_ref, state_ref,
    dq_ref, dk_ref, dv_ref, dke_ref, dve_ref, back_ref,
    kw, vw, dkw, dvw,
):
    tiles = q_ref.shape[0] // TILE
    widen(kw, ke_ref, k_ref)
    widen(vw, ve_ref, v_ref)
    kt = kw[...].T
    causal = causal_t()
    dkw[...] = jnp.zeros_like(dkw)
    dvw[...] = jnp.zeros_like(dvw)
    back = jnp.zeros((DH, DH), F32)
    for i in reversed(range(tiles)):
        rows = slice(i * TILE, (i + 1) * TILE)
        span = slice(i * TILE, i * TILE + SPAN)
        own = slice(LEAD + i * TILE, LEAD + (i + 1) * TILE)
        q, k, v, g = q_ref[rows, :], k_ref[rows, :], v_ref[rows, :], g_ref[rows, :]
        gt = g.astype(F32).T
        normed = norm_ref[0, i]
        delta = jnp.sum(gt * win_ref[0, i], axis=0, keepdims=True)
        inner = jnp.mean(gt * normed, axis=0, keepdims=True)
        gl_f = inv_ref[0, i] * (gt - normed * inner)
        glt = gl_f.astype(BF16)
        gl = gl_f.T.astype(BF16)
        probs = probs_ref[0, i]
        dprob = mm_nt(vw[span, :], g)
        dscore = probs.astype(F32) * ((dprob - delta) * SCALE)
        intra_grad = jnp.where(causal, mm(v, glt), 0.0)
        ds = jnp.concatenate(
            [dscore[:LEAD].astype(BF16), (dscore[LEAD:] + intra_grad).astype(BF16)], axis=0
        )
        intra = jnp.where(causal, mm_nt(k, q), 0.0).astype(BF16)
        rounded = back.astype(BF16)
        dq_ref[rows, :] = (mm(kt[:, span], ds).T + mm(gl, state_ref[0, i])).astype(BF16)
        dkw[span, :] += mm(ds, q)
        dvw[span, :] += mm(probs, g)
        dkw[own, :] += mm(v, rounded)
        dvw[own, :] += mm_nt(k, rounded) + mm(intra, gl)
        back = back + mm(glt, q)
    back_ref[0] = back
    dk_ref[...] = dkw[LEAD:, :]
    dv_ref[...] = dvw[LEAD:, :]
    dke_ref[...] = dkw[LEAD - EDGE : LEAD, :].astype(BF16)
    dve_ref[...] = dvw[LEAD - EDGE : LEAD, :].astype(BF16)


def finish_kernel(k_ref, v_ref, dk_ref, dv_ref, rk_ref, rv_ref, later_ref, gk_ref, gv_ref):
    later = later_ref[0].astype(BF16)
    head = k_ref.shape[0] - EDGE
    dk = dk_ref[...] + mm(v_ref[...], later)
    dv = dv_ref[...] + mm_nt(k_ref[...], later)
    gk_ref[:head, :] = dk[:head].astype(BF16)
    gv_ref[:head, :] = dv[:head].astype(BF16)
    gk_ref[head:, :] = (dk[head:] + rk_ref[...].astype(F32)).astype(BF16)
    gv_ref[head:, :] = (dv[head:] + rv_ref[...].astype(F32)).astype(BF16)


def shifted(shard, by):
    count = lax.axis_size("seq")
    pairs = [(i, i + by) for i in range(count) if 0 <= i + by < count]
    return lax.ppermute(shard, "seq", pairs)


def entering(local, backward):
    count = lax.axis_size("seq")
    place = lax.axis_index("seq")
    gathered = lax.all_gather(local.astype(BF16), "seq")
    order = jnp.arange(count)
    use = order > place if backward else order < place
    return jnp.sum(
        jnp.where(use[:, None, None, None], gathered.astype(F32), 0.0), axis=0
    )


def shards(queries, keys, values, w_out, grad_y):
    tok, width = queries.shape
    groups = width // DH
    tiles = tok // TILE
    place = lax.axis_index("seq")
    tokens_all = tok * lax.axis_size("seq")
    params = pltpu.CompilerParams(
        dimension_semantics=("arbitrary",), vmem_limit_bytes=40 * 1024 * 1024
    )

    def cols(rows):
        return pl.BlockSpec((rows, DH), lambda h: (0, h))

    def heads(*dims):
        return pl.BlockSpec((1,) + dims, lambda h: (h,) + (0,) * len(dims))

    def shape(dims, dtype):
        return jax.ShapeDtypeStruct(dims, dtype)

    def cost(flops, nbytes):
        return pl.CostEstimate(flops=flops, bytes_accessed=nbytes, transcendentals=0)

    ke = shifted(keys[tok - EDGE :], 1)
    ve = shifted(values[tok - EDGE :], 1)
    by_head_k = keys.reshape(tok, groups, DH)
    by_head_v = values.reshape(tok, groups, DH)
    totals = jnp.einsum("thv,thk->hvk", by_head_v, by_head_k, preferred_element_type=F32)
    before = entering(totals, False)
    first = (place * tok).astype(jnp.int32).reshape(1)
    wide = tok + LEAD
    saved = [
        shape((groups, tiles, SPAN, TILE), BF16),
        shape((groups, tiles, DH, TILE), F32),
        shape((groups, tiles, DH, TILE), F32),
        shape((groups, tiles, 1, TILE), F32),
        shape((groups, tiles, DH, DH), BF16),
    ]
    saved_specs = [
        heads(tiles, SPAN, TILE),
        heads(tiles, DH, TILE),
        heads(tiles, DH, TILE),
        heads(tiles, 1, TILE),
        heads(tiles, DH, DH),
    ]
    mixed, *kept = pl.pallas_call(
        forward_kernel,
        grid=(groups,),
        in_specs=[pl.BlockSpec(memory_space=pltpu.SMEM)]
        + [cols(tok)] * 3
        + [cols(EDGE)] * 2
        + [heads(DH, DH)],
        out_specs=[cols(tok)] + saved_specs,
        out_shape=[shape((tok, width), BF16)] + saved,
        scratch_shapes=[pltpu.VMEM((wide, DH), BF16)] * 2,
        compiler_params=params,
        cost_estimate=cost(8 * groups * tok * SPAN * DH, 20 * tok * width),
        name="mixer_forward",
    )(first, queries, keys, values, ke, ve, before)

    grad_full = lax.all_gather(grad_y, "head", axis=1, tiled=True)
    weight = lax.all_gather(w_out, "seq", axis=1, tiled=True)
    weight_part = lax.psum_scatter(
        lax.dot_general(
            grad_full, mixed, (((0,), (0,)), ((), ())), preferred_element_type=F32
        ).astype(BF16),
        "seq",
        scatter_dimension=0,
        tiled=True,
    ).astype(F32)
    projection_sensitivity = weight_part.T * tokens_all ** (-0.5)
    grad_mixed = mm_nt(grad_full, weight).astype(BF16)
    mixer_result = lax.psum_scatter(
        mm(mixed, weight).astype(BF16), "head", scatter_dimension=1, tiled=True
    )

    dq, dk, dv, dke, dve, back = pl.pallas_call(
        backward_kernel,
        grid=(groups,),
        in_specs=[cols(tok)] * 3 + [cols(EDGE)] * 2 + [cols(tok)] + saved_specs,
        out_specs=[cols(tok)] * 3 + [cols(EDGE)] * 2 + [heads(DH, DH)],
        out_shape=[
            shape((tok, width), BF16),
            shape((tok, width), F32),
            shape((tok, width), F32),
            shape((EDGE, width), BF16),
            shape((EDGE, width), BF16),
            shape((groups, DH, DH), F32),
        ],
        scratch_shapes=[pltpu.VMEM((wide, DH), BF16)] * 2 + [pltpu.VMEM((wide, DH), F32)] * 2,
        compiler_params=params,
        cost_estimate=cost(12 * groups * tok * SPAN * DH, 40 * tok * width),
        name="mixer_backward",
    )(queries, keys, values, ke, ve, grad_mixed, *kept)
    rk = shifted(dke, -1)
    rv = shifted(dve, -1)
    later = entering(back, True)
    gk, gv = pl.pallas_call(
        finish_kernel,
        grid=(groups,),
        in_specs=[cols(tok)] * 4 + [cols(EDGE)] * 2 + [heads(DH, DH)],
        out_specs=[cols(tok)] * 2,
        out_shape=[shape((tok, width), BF16)] * 2,
        compiler_params=params,
        cost_estimate=cost(4 * tok * width * DH, 20 * tok * width),
        name="mixer_finish",
    )(keys, values, dk, dv, rk, rv, later)
    return (mixer_result, dq, gk, gv, projection_sensitivity)


def solution(mesh):
    placed = (
        P("seq", "head"),
        P("seq", "head"),
        P("seq", "head"),
        P("head", "seq"),
        P("seq", "head"),
    )
    return jax.shard_map(
        shards,
        mesh=mesh,
        in_specs=placed,
        out_specs=(
            P("seq", "head"),
            P("seq", "head"),
            P("seq", "head"),
            P("seq", "head"),
            P("head", "seq"),
        ),
        check_vma=False,
    )
```

```python
import math

import jax
import jax.numpy as jnp
from jax import lax
from jax.experimental import pallas as pl
from jax.experimental.pallas import tpu as pltpu
from jax.sharding import PartitionSpec as P

DH = 128
BLOCK = 64
BAND = 8
TILE = 128
EDGE = (BAND - 1) * BLOCK
LEAD = BAND * BLOCK
SPAN = LEAD + TILE
EPSILON = 1e-05
MASKED = -1e30
SCALE = 1.0 / math.sqrt(DH)
LOG2E = 1.0 / math.log(2.0)
F32 = jnp.float32
BF16 = jnp.bfloat16


def mm(a, b):
    return jnp.dot(a, b, preferred_element_type=F32)


def mm_nt(a, b):
    return lax.dot_general(a, b, (((1,), (1,)), ((), ())), preferred_element_type=F32)


def widen(wide, edge_ref, own_ref):
    wide[0 : LEAD - EDGE, :] = jnp.zeros((LEAD - EDGE, DH), wide.dtype)
    wide[LEAD - EDGE : LEAD, :] = edge_ref[...]
    wide[LEAD:, :] = own_ref[...]


def causal_t():
    key = lax.broadcasted_iota(jnp.int32, (TILE, TILE), 0)
    query = lax.broadcasted_iota(jnp.int32, (TILE, TILE), 1)
    return key <= query


def forward_kernel(
    first_ref, q_ref, k_ref, v_ref, ke_ref, ve_ref, before_ref,
    mixed_ref, probs_ref, win_ref, norm_ref, inv_ref, state_ref,
    kw, vw,
):
    tiles = q_ref.shape[0] // TILE
    widen(kw, ke_ref, k_ref)
    widen(vw, ve_ref, v_ref)
    vt = vw[...].T
    first = first_ref[0]
    key = lax.broadcasted_iota(jnp.int32, (SPAN, TILE), 0)
    query = lax.broadcasted_iota(jnp.int32, (SPAN, TILE), 1)
    low = (query // BLOCK + 1) * BLOCK
    high = query + LEAD
    causal = causal_t()
    state = before_ref[0]
    for i in range(tiles):
        rows = slice(i * TILE, (i + 1) * TILE)
        q = q_ref[rows, :]
        raw = mm_nt(kw[i * TILE : i * TILE + SPAN, :], q)
        allowed = (key >= jnp.maximum(low, LEAD - i * TILE - first)) & (key <= high)
        score = jnp.where(allowed, raw, MASKED)
        row_max = jnp.max(score, axis=0, keepdims=True)
        raised = jnp.exp2((score - row_max) * (SCALE * LOG2E))
        inv_total = 1.0 / jnp.sum(raised, axis=0, keepdims=True)
        probs = (raised * inv_total).astype(BF16)
        probs_ref[0, i] = probs
        window = mm(vt[:, i * TILE : i * TILE + SPAN], probs)
        vt_own = vt[:, LEAD + i * TILE : LEAD + (i + 1) * TILE]
        intra = jnp.where(causal, raw[LEAD:], 0.0).astype(BF16)
        rounded = state.astype(BF16)
        state_ref[0, i] = rounded
        linear = mm(vt_own, intra) + mm_nt(rounded, q)
        state = state + mm(vt_own, k_ref[rows, :])
        inv = lax.rsqrt(jnp.mean(linear * linear, axis=0, keepdims=True) + EPSILON)
        normed = linear * inv
        win_ref[0, i] = window
        norm_ref[0, i] = normed
        inv_ref[0, i] = inv
        mixed_ref[rows, :] = (normed + window).T.astype(BF16)


def backward_kernel(
    q_ref, k_ref, v_ref, ke_ref, ve_ref, g_ref,
    probs_ref, win_ref, norm_ref, inv_ref, state_ref,
    dq_ref, dk_ref, dv_ref, dke_ref, dve_ref, back_ref,
    kw, vw, dkw, dvw,
):
    tiles = q_ref.shape[0] // TILE
    widen(kw, ke_ref, k_ref)
    widen(vw, ve_ref, v_ref)
    kt = kw[...].T
    causal = causal_t()
    dkw[...] = jnp.zeros_like(dkw)
    dvw[...] = jnp.zeros_like(dvw)
    back = jnp.zeros((DH, DH), F32)
    for i in reversed(range(tiles)):
        rows = slice(i * TILE, (i + 1) * TILE)
        span = slice(i * TILE, i * TILE + SPAN)
        own = slice(LEAD + i * TILE, LEAD + (i + 1) * TILE)
        q, k, v, g = q_ref[rows, :], k_ref[rows, :], v_ref[rows, :], g_ref[rows, :]
        gt = g.astype(F32).T
        normed = norm_ref[0, i]
        delta = jnp.sum(gt * win_ref[0, i], axis=0, keepdims=True)
        inner = jnp.mean(gt * normed, axis=0, keepdims=True)
        gl_f = inv_ref[0, i] * (gt - normed * inner)
        glt = gl_f.astype(BF16)
        gl = gl_f.T.astype(BF16)
        probs = probs_ref[0, i]
        dprob = mm_nt(vw[span, :], g)
        dscore = probs.astype(F32) * ((dprob - delta) * SCALE)
        intra_grad = jnp.where(causal, mm(v, glt), 0.0)
        ds = jnp.concatenate(
            [dscore[:LEAD].astype(BF16), (dscore[LEAD:] + intra_grad).astype(BF16)], axis=0
        )
        intra = jnp.where(causal, mm_nt(k, q), 0.0).astype(BF16)
        rounded = back.astype(BF16)
        dq_ref[rows, :] = (mm(kt[:, span], ds).T + mm(gl, state_ref[0, i])).astype(BF16)
        dkw[span, :] += mm(ds, q)
        dvw[span, :] += mm(probs, g)
        dkw[own, :] += mm(v, rounded)
        dvw[own, :] += mm_nt(k, rounded) + mm(intra, gl)
        back = back + mm(glt, q)
    back_ref[0] = back
    dk_ref[...] = dkw[LEAD:, :]
    dv_ref[...] = dvw[LEAD:, :]
    dke_ref[...] = dkw[LEAD - EDGE : LEAD, :].astype(BF16)
    dve_ref[...] = dvw[LEAD - EDGE : LEAD, :].astype(BF16)


def finish_kernel(k_ref, v_ref, dk_ref, dv_ref, rk_ref, rv_ref, later_ref, gk_ref, gv_ref):
    later = later_ref[0].astype(BF16)
    head = k_ref.shape[0] - EDGE
    dk = dk_ref[...] + mm(v_ref[...], later)
    dv = dv_ref[...] + mm_nt(k_ref[...], later)
    gk_ref[:head, :] = dk[:head].astype(BF16)
    gv_ref[:head, :] = dv[:head].astype(BF16)
    gk_ref[head:, :] = (dk[head:] + rk_ref[...].astype(F32)).astype(BF16)
    gv_ref[head:, :] = (dv[head:] + rv_ref[...].astype(F32)).astype(BF16)


def shifted(shard, by):
    count = lax.axis_size("seq")
    pairs = [(i, i + by) for i in range(count) if 0 <= i + by < count]
    return lax.ppermute(shard, "seq", pairs)


def entering(local, backward):
    count = lax.axis_size("seq")
    inclusive = local
    exclusive = jnp.zeros_like(local)
    step = 1
    while step < count:
        arrived = shifted(inclusive.astype(BF16), -step if backward else step).astype(F32)
        exclusive = exclusive + arrived
        inclusive = inclusive + arrived
        step *= 2
    return exclusive


def ring_order(count):
    return list(range(0, count, 2)) + list(range(count - 1, 0, -2))


def ring_place(index, count):
    return jnp.where(index % 2 == 0, index // 2, count - 1 - index // 2)


def ring_owner(place, count):
    place = lax.rem(place + 2 * count, count)
    return jnp.where(place < count // 2, 2 * place, 2 * (count - 1 - place) + 1)


def ring_step(block, way):
    count = lax.axis_size("seq")
    ring = ring_order(count)
    pairs = [(ring[i], ring[(i + way) % count]) for i in range(count)]
    return lax.ppermute(block, "seq", pairs)


def ring_gather(block):
    count = lax.axis_size("seq")
    index = lax.axis_index("seq")
    place = ring_place(index, count)
    rows, cols = block.shape
    half = rows // 2
    whole = jnp.zeros((rows, cols * count), block.dtype)
    whole = lax.dynamic_update_slice(whole, block, (0, index * cols))
    up, down = block[:half], block[half:]
    for t in range(1, count):
        up = ring_step(up, 1)
        down = ring_step(down, -1)
        whole = lax.dynamic_update_slice(whole, up, (0, ring_owner(place - t, count) * cols))
        whole = lax.dynamic_update_slice(whole, down, (half, ring_owner(place + t, count) * cols))
    return whole


def ring_scatter(parts):
    count = lax.axis_size("seq")
    place = ring_place(lax.axis_index("seq"), count)
    rows = parts.shape[0] // count
    half = rows // 2

    def piece(at, lower):
        start = ring_owner(at, count) * rows + lower * half
        return lax.dynamic_slice_in_dim(parts, start, half, 0)

    up, down = piece(place - 1, 0), piece(place + 1, 1)
    for t in range(count - 1):
        up = ring_step(up, 1).astype(F32) + piece(place - 2 - t, 0).astype(F32)
        down = ring_step(down, -1).astype(F32) + piece(place + 2 + t, 1).astype(F32)
        if t < count - 2:
            up, down = up.astype(BF16), down.astype(BF16)
    return jnp.concatenate([up, down], axis=0)


def shards(queries, keys, values, w_out, grad_y):
    tok, width = queries.shape
    groups = width // DH
    tiles = tok // TILE
    place = lax.axis_index("seq")
    tokens_all = tok * lax.axis_size("seq")
    params = pltpu.CompilerParams(
        dimension_semantics=("arbitrary",), vmem_limit_bytes=40 * 1024 * 1024
    )

    def cols(rows):
        return pl.BlockSpec((rows, DH), lambda h: (0, h))

    def heads(*dims):
        return pl.BlockSpec((1,) + dims, lambda h: (h,) + (0,) * len(dims))

    def shape(dims, dtype):
        return jax.ShapeDtypeStruct(dims, dtype)

    def cost(flops, nbytes):
        return pl.CostEstimate(flops=flops, bytes_accessed=nbytes, transcendentals=0)

    ke = shifted(keys[tok - EDGE :], 1)
    ve = shifted(values[tok - EDGE :], 1)
    by_head_k = keys.reshape(tok, groups, DH)
    by_head_v = values.reshape(tok, groups, DH)
    totals = jnp.einsum("thv,thk->hvk", by_head_v, by_head_k, preferred_element_type=F32)
    before = entering(totals, False)
    first = (place * tok).astype(jnp.int32).reshape(1)
    wide = tok + LEAD
    saved = [
        shape((groups, tiles, SPAN, TILE), BF16),
        shape((groups, tiles, DH, TILE), F32),
        shape((groups, tiles, DH, TILE), F32),
        shape((groups, tiles, 1, TILE), F32),
        shape((groups, tiles, DH, DH), BF16),
    ]
    saved_specs = [
        heads(tiles, SPAN, TILE),
        heads(tiles, DH, TILE),
        heads(tiles, DH, TILE),
        heads(tiles, 1, TILE),
        heads(tiles, DH, DH),
    ]
    mixed, *kept = pl.pallas_call(
        forward_kernel,
        grid=(groups,),
        in_specs=[pl.BlockSpec(memory_space=pltpu.SMEM)]
        + [cols(tok)] * 3
        + [cols(EDGE)] * 2
        + [heads(DH, DH)],
        out_specs=[cols(tok)] + saved_specs,
        out_shape=[shape((tok, width), BF16)] + saved,
        scratch_shapes=[pltpu.VMEM((wide, DH), BF16)] * 2,
        compiler_params=params,
        cost_estimate=cost(8 * groups * tok * SPAN * DH, 20 * tok * width),
        name="mixer_forward",
    )(first, queries, keys, values, ke, ve, before)

    grad_full = lax.all_gather(grad_y, "head", axis=1, tiled=True)
    weight = ring_gather(w_out)
    weight_part = ring_scatter(
        lax.dot_general(
            grad_full, mixed, (((0,), (0,)), ((), ())), preferred_element_type=F32
        ).astype(BF16)
    )
    projection_sensitivity = weight_part.T * tokens_all ** (-0.5)
    grad_mixed = mm_nt(grad_full, weight).astype(BF16)
    mixer_result = lax.psum_scatter(
        mm(mixed, weight).astype(BF16), "head", scatter_dimension=1, tiled=True
    )

    dq, dk, dv, dke, dve, back = pl.pallas_call(
        backward_kernel,
        grid=(groups,),
        in_specs=[cols(tok)] * 3 + [cols(EDGE)] * 2 + [cols(tok)] + saved_specs,
        out_specs=[cols(tok)] * 3 + [cols(EDGE)] * 2 + [heads(DH, DH)],
        out_shape=[
            shape((tok, width), BF16),
            shape((tok, width), F32),
            shape((tok, width), F32),
            shape((EDGE, width), BF16),
            shape((EDGE, width), BF16),
            shape((groups, DH, DH), F32),
        ],
        scratch_shapes=[pltpu.VMEM((wide, DH), BF16)] * 2 + [pltpu.VMEM((wide, DH), F32)] * 2,
        compiler_params=params,
        cost_estimate=cost(12 * groups * tok * SPAN * DH, 40 * tok * width),
        name="mixer_backward",
    )(queries, keys, values, ke, ve, grad_mixed, *kept)
    rk = shifted(dke, -1)
    rv = shifted(dve, -1)
    later = entering(back, True)
    gk, gv = pl.pallas_call(
        finish_kernel,
        grid=(groups,),
        in_specs=[cols(tok)] * 4 + [cols(EDGE)] * 2 + [heads(DH, DH)],
        out_specs=[cols(tok)] * 2,
        out_shape=[shape((tok, width), BF16)] * 2,
        compiler_params=params,
        cost_estimate=cost(4 * tok * width * DH, 20 * tok * width),
        name="mixer_finish",
    )(keys, values, dk, dv, rk, rv, later)
    return (mixer_result, dq, gk, gv, projection_sensitivity)


def solution(mesh):
    placed = (
        P("seq", "head"),
        P("seq", "head"),
        P("seq", "head"),
        P("head", "seq"),
        P("seq", "head"),
    )
    return jax.shard_map(
        shards,
        mesh=mesh,
        in_specs=placed,
        out_specs=(
            P("seq", "head"),
            P("seq", "head"),
            P("seq", "head"),
            P("seq", "head"),
            P("head", "seq"),
        ),
        check_vma=False,
    )
```

```python
import math

import jax
import jax.numpy as jnp
from jax import lax
from jax.experimental import pallas as pl
from jax.experimental.pallas import tpu as pltpu
from jax.sharding import PartitionSpec as P

DH = 128
BLOCK = 64
BAND = 8
TILE = 128
EDGE = (BAND - 1) * BLOCK
LEAD = BAND * BLOCK
SPAN = LEAD + TILE
EPSILON = 1e-05
MASKED = -1e30
SCALE = 1.0 / math.sqrt(DH)
LOG2E = 1.0 / math.log(2.0)
F32 = jnp.float32
BF16 = jnp.bfloat16


def mm(a, b):
    return jnp.dot(a, b, preferred_element_type=F32)


def mm_nt(a, b):
    return lax.dot_general(a, b, (((1,), (1,)), ((), ())), preferred_element_type=F32)


def widen(wide, edge_ref, own_ref):
    wide[0 : LEAD - EDGE, :] = jnp.zeros((LEAD - EDGE, DH), wide.dtype)
    wide[LEAD - EDGE : LEAD, :] = edge_ref[...]
    wide[LEAD:, :] = own_ref[...]


def causal_t():
    key = lax.broadcasted_iota(jnp.int32, (TILE, TILE), 0)
    query = lax.broadcasted_iota(jnp.int32, (TILE, TILE), 1)
    return key <= query


def forward_kernel(
    first_ref, q_ref, k_ref, v_ref, ke_ref, ve_ref, before_ref,
    mixed_ref, probs_ref, win_ref, norm_ref, inv_ref, state_ref,
    kw, vw,
):
    tiles = q_ref.shape[0] // TILE
    widen(kw, ke_ref, k_ref)
    widen(vw, ve_ref, v_ref)
    vt = vw[...].T
    first = first_ref[0]
    key = lax.broadcasted_iota(jnp.int32, (SPAN, TILE), 0)
    query = lax.broadcasted_iota(jnp.int32, (SPAN, TILE), 1)
    low = (query // BLOCK + 1) * BLOCK
    high = query + LEAD
    causal = causal_t()
    state = before_ref[0]
    for i in range(tiles):
        rows = slice(i * TILE, (i + 1) * TILE)
        q = q_ref[rows, :]
        raw = mm_nt(kw[i * TILE : i * TILE + SPAN, :], q)
        allowed = (key >= jnp.maximum(low, LEAD - i * TILE - first)) & (key <= high)
        score = jnp.where(allowed, raw, MASKED)
        row_max = jnp.max(score, axis=0, keepdims=True)
        raised = jnp.exp2((score - row_max) * (SCALE * LOG2E))
        inv_total = 1.0 / jnp.sum(raised, axis=0, keepdims=True)
        probs = (raised * inv_total).astype(BF16)
        probs_ref[0, i] = probs
        window = mm(vt[:, i * TILE : i * TILE + SPAN], probs)
        vt_own = vt[:, LEAD + i * TILE : LEAD + (i + 1) * TILE]
        intra = jnp.where(causal, raw[LEAD:], 0.0).astype(BF16)
        rounded = state.astype(BF16)
        state_ref[0, i] = rounded
        linear = mm(vt_own, intra) + mm_nt(rounded, q)
        state = state + mm(vt_own, k_ref[rows, :])
        inv = lax.rsqrt(jnp.mean(linear * linear, axis=0, keepdims=True) + EPSILON)
        normed = linear * inv
        win_ref[0, i] = window
        norm_ref[0, i] = normed
        inv_ref[0, i] = inv
        mixed_ref[rows, :] = (normed + window).T.astype(BF16)


def backward_kernel(
    q_ref, k_ref, v_ref, ke_ref, ve_ref, g_ref,
    probs_ref, win_ref, norm_ref, inv_ref, state_ref,
    dq_ref, dk_ref, dv_ref, dke_ref, dve_ref, back_ref,
    kw, vw, dkw, dvw,
):
    tiles = q_ref.shape[0] // TILE
    widen(kw, ke_ref, k_ref)
    widen(vw, ve_ref, v_ref)
    kt = kw[...].T
    causal = causal_t()
    dkw[...] = jnp.zeros_like(dkw)
    dvw[...] = jnp.zeros_like(dvw)
    back = jnp.zeros((DH, DH), F32)
    for i in reversed(range(tiles)):
        rows = slice(i * TILE, (i + 1) * TILE)
        span = slice(i * TILE, i * TILE + SPAN)
        own = slice(LEAD + i * TILE, LEAD + (i + 1) * TILE)
        q, k, v, g = q_ref[rows, :], k_ref[rows, :], v_ref[rows, :], g_ref[rows, :]
        gt = g.astype(F32).T
        normed = norm_ref[0, i]
        delta = jnp.sum(gt * win_ref[0, i], axis=0, keepdims=True)
        inner = jnp.mean(gt * normed, axis=0, keepdims=True)
        gl_f = inv_ref[0, i] * (gt - normed * inner)
        glt = gl_f.astype(BF16)
        gl = gl_f.T.astype(BF16)
        probs = probs_ref[0, i]
        dprob = mm_nt(vw[span, :], g)
        dscore = probs.astype(F32) * ((dprob - delta) * SCALE)
        intra_grad = jnp.where(causal, mm(v, glt), 0.0)
        ds = jnp.concatenate(
            [dscore[:LEAD].astype(BF16), (dscore[LEAD:] + intra_grad).astype(BF16)], axis=0
        )
        intra = jnp.where(causal, mm_nt(k, q), 0.0).astype(BF16)
        rounded = back.astype(BF16)
        dq_ref[rows, :] = (mm(kt[:, span], ds).T + mm(gl, state_ref[0, i])).astype(BF16)
        dkw[span, :] += mm(ds, q)
        dvw[span, :] += mm(probs, g)
        dkw[own, :] += mm(v, rounded)
        dvw[own, :] += mm_nt(k, rounded) + mm(intra, gl)
        back = back + mm(glt, q)
    back_ref[0] = back
    dk_ref[...] = dkw[LEAD:, :]
    dv_ref[...] = dvw[LEAD:, :]
    dke_ref[...] = dkw[LEAD - EDGE : LEAD, :].astype(BF16)
    dve_ref[...] = dvw[LEAD - EDGE : LEAD, :].astype(BF16)


def finish_kernel(k_ref, v_ref, dk_ref, dv_ref, rk_ref, rv_ref, later_ref, gk_ref, gv_ref):
    later = later_ref[0].astype(BF16)
    head = k_ref.shape[0] - EDGE
    dk = dk_ref[...] + mm(v_ref[...], later)
    dv = dv_ref[...] + mm_nt(k_ref[...], later)
    gk_ref[:head, :] = dk[:head].astype(BF16)
    gv_ref[:head, :] = dv[:head].astype(BF16)
    gk_ref[head:, :] = (dk[head:] + rk_ref[...].astype(F32)).astype(BF16)
    gv_ref[head:, :] = (dv[head:] + rv_ref[...].astype(F32)).astype(BF16)


def shifted(shard, by):
    count = lax.axis_size("seq")
    pairs = [(i, i + by) for i in range(count) if 0 <= i + by < count]
    return lax.ppermute(shard, "seq", pairs)


def entering(local, backward):
    count = lax.axis_size("seq")
    inclusive = local
    exclusive = jnp.zeros_like(local)
    step = 1
    while step < count:
        arrived = shifted(inclusive.astype(BF16), -step if backward else step).astype(F32)
        exclusive = exclusive + arrived
        inclusive = inclusive + arrived
        step *= 2
    return exclusive


def ring_order(count):
    return list(range(0, count, 2)) + list(range(count - 1, 0, -2))


def ring_place(index, count):
    return jnp.where(index % 2 == 0, index // 2, count - 1 - index // 2)


def ring_owner(place, count):
    place = lax.rem(place + 2 * count, count)
    return jnp.where(place < count // 2, 2 * place, 2 * (count - 1 - place) + 1)


def ring_step(block, way):
    count = lax.axis_size("seq")
    ring = ring_order(count)
    pairs = [(ring[i], ring[(i + way) % count]) for i in range(count)]
    return lax.ppermute(block, "seq", pairs)


def ring_gather(block, after):
    count = lax.axis_size("seq")
    index = lax.axis_index("seq")
    place = ring_place(index, count)
    rows, cols = block.shape
    half = rows // 2
    whole = jnp.zeros((rows, cols * count), block.dtype)
    whole = lax.dynamic_update_slice(whole, block, (0, index * cols))
    up, down = block[:half], block[half:]
    for t in range(1, count):
        if 2 <= t < 2 + len(after):
            up, down, _ = lax.optimization_barrier((up, down, after[t - 2]))
        up = ring_step(up, 1)
        down = ring_step(down, -1)
        whole = lax.dynamic_update_slice(whole, up, (0, ring_owner(place - t, count) * cols))
        whole = lax.dynamic_update_slice(whole, down, (half, ring_owner(place + t, count) * cols))
    return whole


def ring_scatter(parts, after):
    count = lax.axis_size("seq")
    place = ring_place(lax.axis_index("seq"), count)
    rows = parts.shape[0] // count
    part = rows // 4

    def piece(at, number):
        start = ring_owner(at, count) * rows + number * part
        return lax.dynamic_slice_in_dim(parts, start, part, 0)

    ways = (1, -1, 1, -1)
    sums = [piece(place - way, number) for number, way in enumerate(ways)]
    for t in range(count - 1):
        if t in after:
            *sums, _ = lax.optimization_barrier((*sums, after[t]))
        source = parts
        for number, way in enumerate(ways):
            arrived = ring_step(sums[number], way).astype(F32)
            start = ring_owner(place - way * (2 + t), count) * rows + number * part
            total = arrived + lax.dynamic_slice_in_dim(source, start, part, 0).astype(F32)
            sums[number] = total.astype(BF16) if t < count - 2 else total
            if number == 1 and t < count - 2:
                source, _ = lax.optimization_barrier((parts, sums[0]))
    return jnp.concatenate(sums, axis=0)


def shards(queries, keys, values, w_out, grad_y):
    tok, width = queries.shape
    groups = width // DH
    tiles = tok // TILE
    place = lax.axis_index("seq")
    tokens_all = tok * lax.axis_size("seq")
    params = pltpu.CompilerParams(
        dimension_semantics=("arbitrary",), vmem_limit_bytes=40 * 1024 * 1024
    )

    def cols(rows, skip=0):
        return pl.BlockSpec((rows, DH), lambda h: (0, h + skip))

    def heads(*dims):
        return pl.BlockSpec((1,) + dims, lambda h: (h,) + (0,) * len(dims))

    def shape(dims, dtype):
        return jax.ShapeDtypeStruct(dims, dtype)

    def cost(flops, nbytes):
        return pl.CostEstimate(flops=flops, bytes_accessed=nbytes, transcendentals=0)

    count = 2
    part = groups // count
    spans = [slice(c * part * DH, (c + 1) * part * DH) for c in range(count)]
    by_head_k = keys.reshape(tok, groups, DH)
    by_head_v = values.reshape(tok, groups, DH)
    totals = jnp.einsum("thv,thk->hvk", by_head_v, by_head_k, preferred_element_type=F32)
    before = entering(totals, False)
    halo = [(shifted(keys[tok - EDGE :, c], 1), shifted(values[tok - EDGE :, c], 1)) for c in spans]
    first = (place * tok).astype(jnp.int32).reshape(1)
    wide = tok + LEAD
    saved = [
        shape((part, tiles, SPAN, TILE), BF16),
        shape((part, tiles, DH, TILE), F32),
        shape((part, tiles, DH, TILE), F32),
        shape((part, tiles, 1, TILE), F32),
        shape((part, tiles, DH, DH), BF16),
    ]
    saved_specs = [
        heads(tiles, SPAN, TILE),
        heads(tiles, DH, TILE),
        heads(tiles, DH, TILE),
        heads(tiles, 1, TILE),
        heads(tiles, DH, DH),
    ]
    grad_full = lax.all_gather(grad_y, "head", axis=1, tiled=True)
    weight = ring_gather(w_out, [halo[0], (halo[1], before)])

    mixed_parts, kept = [], []
    for c in range(count):
        skip = c * part
        mixed_part, *rest = pl.pallas_call(
            forward_kernel,
            grid=(part,),
            in_specs=[pl.BlockSpec(memory_space=pltpu.SMEM)]
            + [cols(tok, skip)] * 3
            + [cols(EDGE)] * 2
            + [pl.BlockSpec((1, DH, DH), lambda h, skip=skip: (h + skip, 0, 0))],
            out_specs=[cols(tok)] + saved_specs,
            out_shape=[shape((tok, part * DH), BF16)] + saved,
            scratch_shapes=[pltpu.VMEM((wide, DH), BF16)] * 2,
            compiler_params=params,
            cost_estimate=cost(24 * part * tok * SPAN * DH, 20 * tok * part * DH),
            name="mixer_forward",
        )(first, queries, keys, values, *halo[c], before)
        mixed_parts.append(mixed_part)
        kept.append(rest)
    mixed = jnp.concatenate(mixed_parts, axis=1)

    weight_terms = lax.dot_general(
        grad_full, mixed, (((0,), (0,)), ((), ())), preferred_element_type=F32
    ).astype(BF16)
    weight, _ = lax.optimization_barrier((weight, weight_terms))
    grad_mixed = mm_nt(grad_full, weight).astype(BF16)

    back_parts = []
    for c in range(count):
        skip = c * part
        back_parts.append(
            pl.pallas_call(
                backward_kernel,
                grid=(part,),
                in_specs=[cols(tok, skip)] * 3
                + [cols(EDGE)] * 2
                + [cols(tok, skip)]
                + saved_specs,
                out_specs=[cols(tok)] * 3 + [cols(EDGE)] * 2 + [heads(DH, DH)],
                out_shape=[
                    shape((tok, part * DH), BF16),
                    shape((tok, part * DH), F32),
                    shape((tok, part * DH), F32),
                    shape((EDGE, part * DH), BF16),
                    shape((EDGE, part * DH), BF16),
                    shape((part, DH, DH), F32),
                ],
                scratch_shapes=[pltpu.VMEM((wide, DH), BF16)] * 2
                + [pltpu.VMEM((wide, DH), F32)] * 2,
                compiler_params=params,
                cost_estimate=cost(24 * part * tok * SPAN * DH, 40 * tok * part * DH),
                name="mixer_backward",
            )(queries, keys, values, *halo[c], grad_mixed, *kept[c])
        )
    dq = jnp.concatenate([p[0] for p in back_parts], axis=1)
    returned = [(shifted(p[3], -1), shifted(p[4], -1)) for p in back_parts]
    weight_part = ring_scatter(weight_terms, {4: returned[0], 5: returned[1]})
    projection_sensitivity = weight_part.T * tokens_all ** (-0.5)
    later = entering(jnp.concatenate([p[5] for p in back_parts], axis=0), True)
    mixed_late, _ = lax.optimization_barrier((mixed, back_parts[-1][5]))
    mixer_result = lax.psum_scatter(
        mm(mixed_late, weight).astype(BF16), "head", scatter_dimension=1, tiled=True
    )
    done = []
    for c in range(count):
        skip = c * part
        done.append(
            pl.pallas_call(
                finish_kernel,
                grid=(part,),
                in_specs=[cols(tok, skip)] * 2
                + [cols(tok)] * 2
                + [cols(EDGE)] * 2
                + [pl.BlockSpec((1, DH, DH), lambda h, skip=skip: (h + skip, 0, 0))],
                out_specs=[cols(tok)] * 2,
                out_shape=[shape((tok, part * DH), BF16)] * 2,
                compiler_params=params,
                cost_estimate=cost(4 * tok * part * DH * DH, 20 * tok * part * DH),
                name="mixer_finish",
            )(keys, values, back_parts[c][1], back_parts[c][2], *returned[c], later)
        )
    gk = jnp.concatenate([d[0] for d in done], axis=1)
    gv = jnp.concatenate([d[1] for d in done], axis=1)
    return (mixer_result, dq, gk, gv, projection_sensitivity)


def solution(mesh):
    placed = (
        P("seq", "head"),
        P("seq", "head"),
        P("seq", "head"),
        P("head", "seq"),
        P("seq", "head"),
    )
    return jax.shard_map(
        shards,
        mesh=mesh,
        in_specs=placed,
        out_specs=(
            P("seq", "head"),
            P("seq", "head"),
            P("seq", "head"),
            P("seq", "head"),
            P("head", "seq"),
        ),
        check_vma=False,
    )
```

```python
import math

import jax
import jax.numpy as jnp
from jax import lax
from jax.experimental import pallas as pl
from jax.experimental.pallas import tpu as pltpu
from jax.sharding import PartitionSpec as P

DH = 128
BLOCK = 64
BAND = 8
TILE = 128
EDGE = (BAND - 1) * BLOCK
LEAD = BAND * BLOCK
SPAN = LEAD + TILE
EPSILON = 1e-05
MASKED = -1e30
SCALE = 1.0 / math.sqrt(DH)
LOG2E = 1.0 / math.log(2.0)
F32 = jnp.float32
BF16 = jnp.bfloat16


def mm(a, b):
    return jnp.dot(a, b, preferred_element_type=F32)


def mm_nt(a, b):
    return lax.dot_general(a, b, (((1,), (1,)), ((), ())), preferred_element_type=F32)


def widen(wide, edge_ref, own_ref):
    wide[0 : LEAD - EDGE, :] = jnp.zeros((LEAD - EDGE, DH), wide.dtype)
    wide[LEAD - EDGE : LEAD, :] = edge_ref[...]
    wide[LEAD:, :] = own_ref[...]


def causal_t():
    key = lax.broadcasted_iota(jnp.int32, (TILE, TILE), 0)
    query = lax.broadcasted_iota(jnp.int32, (TILE, TILE), 1)
    return key <= query


def forward_kernel(
    first_ref, q_ref, k_ref, v_ref, ke_ref, ve_ref, before_ref,
    mixed_ref, probs_ref, win_ref, norm_ref, inv_ref, state_ref,
    kw, vw,
):
    tiles = q_ref.shape[0] // TILE
    widen(kw, ke_ref, k_ref)
    widen(vw, ve_ref, v_ref)
    vt = vw[...].T
    first = first_ref[0]
    key = lax.broadcasted_iota(jnp.int32, (SPAN, TILE), 0)
    query = lax.broadcasted_iota(jnp.int32, (SPAN, TILE), 1)
    low = (query // BLOCK + 1) * BLOCK
    high = query + LEAD
    causal = causal_t()
    state = before_ref[0]
    for i in range(tiles):
        rows = slice(i * TILE, (i + 1) * TILE)
        q = q_ref[rows, :]
        raw = mm_nt(kw[i * TILE : i * TILE + SPAN, :], q)
        allowed = (key >= jnp.maximum(low, LEAD - i * TILE - first)) & (key <= high)
        score = jnp.where(allowed, raw, MASKED)
        row_max = jnp.max(score, axis=0, keepdims=True)
        raised = jnp.exp2((score - row_max) * (SCALE * LOG2E))
        inv_total = 1.0 / jnp.sum(raised, axis=0, keepdims=True)
        probs = (raised * inv_total).astype(BF16)
        probs_ref[0, i] = probs
        window = mm(vt[:, i * TILE : i * TILE + SPAN], probs)
        vt_own = vt[:, LEAD + i * TILE : LEAD + (i + 1) * TILE]
        intra = jnp.where(causal, raw[LEAD:], 0.0).astype(BF16)
        rounded = state.astype(BF16)
        state_ref[0, i] = rounded
        linear = mm(vt_own, intra) + mm_nt(rounded, q)
        state = state + mm(vt_own, k_ref[rows, :])
        inv = lax.rsqrt(jnp.mean(linear * linear, axis=0, keepdims=True) + EPSILON)
        normed = linear * inv
        win_ref[0, i] = window
        norm_ref[0, i] = normed
        inv_ref[0, i] = inv
        mixed_ref[rows, :] = (normed + window).T.astype(BF16)


def backward_kernel(
    q_ref, k_ref, v_ref, ke_ref, ve_ref, g_ref,
    probs_ref, win_ref, norm_ref, inv_ref, state_ref,
    dq_ref, dk_ref, dv_ref, dke_ref, dve_ref, back_ref,
    kw, vw, dkw, dvw,
):
    tiles = q_ref.shape[0] // TILE
    widen(kw, ke_ref, k_ref)
    widen(vw, ve_ref, v_ref)
    kt = kw[...].T
    causal = causal_t()
    dkw[...] = jnp.zeros_like(dkw)
    dvw[...] = jnp.zeros_like(dvw)
    back = jnp.zeros((DH, DH), F32)
    for i in reversed(range(tiles)):
        rows = slice(i * TILE, (i + 1) * TILE)
        span = slice(i * TILE, i * TILE + SPAN)
        own = slice(LEAD + i * TILE, LEAD + (i + 1) * TILE)
        q, k, v, g = q_ref[rows, :], k_ref[rows, :], v_ref[rows, :], g_ref[rows, :]
        gt = g.astype(F32).T
        normed = norm_ref[0, i]
        delta = jnp.sum(gt * win_ref[0, i], axis=0, keepdims=True)
        inner = jnp.mean(gt * normed, axis=0, keepdims=True)
        gl_f = inv_ref[0, i] * (gt - normed * inner)
        glt = gl_f.astype(BF16)
        gl = gl_f.T.astype(BF16)
        probs = probs_ref[0, i]
        dprob = mm_nt(vw[span, :], g)
        dscore = probs.astype(F32) * ((dprob - delta) * SCALE)
        intra_grad = jnp.where(causal, mm(v, glt), 0.0)
        ds = jnp.concatenate(
            [dscore[:LEAD].astype(BF16), (dscore[LEAD:] + intra_grad).astype(BF16)], axis=0
        )
        intra = jnp.where(causal, mm_nt(k, q), 0.0).astype(BF16)
        rounded = back.astype(BF16)
        dq_ref[rows, :] = (mm(kt[:, span], ds).T + mm(gl, state_ref[0, i])).astype(BF16)
        dkw[span, :] += mm(ds, q)
        dvw[span, :] += mm(probs, g)
        dkw[own, :] += mm(v, rounded)
        dvw[own, :] += mm_nt(k, rounded) + mm(intra, gl)
        back = back + mm(glt, q)
    back_ref[0] = back
    dk_ref[...] = dkw[LEAD:, :]
    dv_ref[...] = dvw[LEAD:, :]
    dke_ref[...] = dkw[LEAD - EDGE : LEAD, :].astype(BF16)
    dve_ref[...] = dvw[LEAD - EDGE : LEAD, :].astype(BF16)


def finish_kernel(k_ref, v_ref, dk_ref, dv_ref, rk_ref, rv_ref, later_ref, gk_ref, gv_ref):
    later = later_ref[0].astype(BF16)
    head = k_ref.shape[0] - EDGE
    dk = dk_ref[...] + mm(v_ref[...], later)
    dv = dv_ref[...] + mm_nt(k_ref[...], later)
    gk_ref[:head, :] = dk[:head].astype(BF16)
    gv_ref[:head, :] = dv[:head].astype(BF16)
    gk_ref[head:, :] = (dk[head:] + rk_ref[...].astype(F32)).astype(BF16)
    gv_ref[head:, :] = (dv[head:] + rv_ref[...].astype(F32)).astype(BF16)


def shifted(shard, by):
    count = lax.axis_size("seq")
    pairs = [(i, i + by) for i in range(count) if 0 <= i + by < count]
    return lax.ppermute(shard, "seq", pairs)


def entering(local, backward):
    count = lax.axis_size("seq")
    inclusive = local
    exclusive = jnp.zeros_like(local)
    step = 1
    while step < count:
        arrived = shifted(inclusive.astype(BF16), -step if backward else step).astype(F32)
        exclusive = exclusive + arrived
        inclusive = inclusive + arrived
        step *= 2
    return exclusive


def ring_order(count):
    return list(range(0, count, 2)) + list(range(count - 1, 0, -2))


def ring_place(index, count):
    return jnp.where(index % 2 == 0, index // 2, count - 1 - index // 2)


def ring_owner(place, count):
    place = lax.rem(place + 2 * count, count)
    return jnp.where(place < count // 2, 2 * place, 2 * (count - 1 - place) + 1)


def ring_step(block, way):
    count = lax.axis_size("seq")
    ring = ring_order(count)
    pairs = [(ring[i], ring[(i + way) % count]) for i in range(count)]
    return lax.ppermute(block, "seq", pairs)


def ring_gather(block, after):
    count = lax.axis_size("seq")
    index = lax.axis_index("seq")
    place = ring_place(index, count)
    rows, cols = block.shape
    half = rows // 2
    whole = jnp.zeros((rows, cols * count), block.dtype)
    whole = lax.dynamic_update_slice(whole, block, (0, index * cols))
    up, down = block[:half], block[half:]
    for t in range(1, count):
        if t in after:
            up, down, _ = lax.optimization_barrier((up, down, after[t]))
        up = ring_step(up, 1)
        down = ring_step(down, -1)
        whole = lax.dynamic_update_slice(whole, up, (0, ring_owner(place - t, count) * cols))
        whole = lax.dynamic_update_slice(whole, down, (half, ring_owner(place + t, count) * cols))
    return whole


def ring_scatter(parts):
    count = lax.axis_size("seq")
    place = ring_place(lax.axis_index("seq"), count)
    rows = parts.shape[0] // count
    half = rows // 2

    def piece(at, lower):
        start = ring_owner(at, count) * rows + lower * half
        return lax.dynamic_slice_in_dim(parts, start, half, 0)

    up, down = piece(place - 1, 0), piece(place + 1, 1)
    for t in range(count - 1):
        up = ring_step(up, 1).astype(F32) + piece(place - 2 - t, 0).astype(F32)
        down = ring_step(down, -1).astype(F32) + piece(place + 2 + t, 1).astype(F32)
        if t < count - 2:
            up, down = up.astype(BF16), down.astype(BF16)
        if t == 1:
            early = (up, down)
    return jnp.concatenate([up, down], axis=0), early


def shards(queries, keys, values, w_out, grad_y):
    tok, width = queries.shape
    groups = width // DH
    tiles = tok // TILE
    place = lax.axis_index("seq")
    tokens_all = tok * lax.axis_size("seq")
    params = pltpu.CompilerParams(
        dimension_semantics=("arbitrary",), vmem_limit_bytes=40 * 1024 * 1024
    )

    def cols(rows, skip=0):
        return pl.BlockSpec((rows, DH), lambda h: (0, h + skip))

    def heads(*dims):
        return pl.BlockSpec((1,) + dims, lambda h: (h,) + (0,) * len(dims))

    def shape(dims, dtype):
        return jax.ShapeDtypeStruct(dims, dtype)

    def cost(flops, nbytes):
        return pl.CostEstimate(flops=flops, bytes_accessed=nbytes, transcendentals=0)

    count = 2
    part = groups // count
    spans = [slice(c * part * DH, (c + 1) * part * DH) for c in range(count)]
    by_head_k = keys.reshape(tok, groups, DH)
    by_head_v = values.reshape(tok, groups, DH)
    totals = jnp.einsum("thv,thk->hvk", by_head_v, by_head_k, preferred_element_type=F32)
    before = entering(totals, False)
    halo = [(shifted(keys[tok - EDGE :, c], 1), shifted(values[tok - EDGE :, c], 1)) for c in spans]
    first = (place * tok).astype(jnp.int32).reshape(1)
    wide = tok + LEAD
    saved = [
        shape((part, tiles, SPAN, TILE), BF16),
        shape((part, tiles, DH, TILE), F32),
        shape((part, tiles, DH, TILE), F32),
        shape((part, tiles, 1, TILE), F32),
        shape((part, tiles, DH, DH), BF16),
    ]
    saved_specs = [
        heads(tiles, SPAN, TILE),
        heads(tiles, DH, TILE),
        heads(tiles, DH, TILE),
        heads(tiles, 1, TILE),
        heads(tiles, DH, DH),
    ]
    grad_full = lax.all_gather(grad_y, "head", axis=1, tiled=True)

    mixed_parts, kept = [], []
    for c in range(count):
        skip = c * part
        mixed_part, *rest = pl.pallas_call(
            forward_kernel,
            grid=(part,),
            in_specs=[pl.BlockSpec(memory_space=pltpu.SMEM)]
            + [cols(tok, skip)] * 3
            + [cols(EDGE)] * 2
            + [pl.BlockSpec((1, DH, DH), lambda h, skip=skip: (h + skip, 0, 0))],
            out_specs=[cols(tok)] + saved_specs,
            out_shape=[shape((tok, part * DH), BF16)] + saved,
            scratch_shapes=[pltpu.VMEM((wide, DH), BF16)] * 2,
            compiler_params=params,
            cost_estimate=cost(24 * part * tok * SPAN * DH, 20 * tok * part * DH),
            name="mixer_forward",
        )(first, queries, keys, values, *halo[c], before)
        mixed_parts.append(mixed_part)
        kept.append(rest)
    mixed = jnp.concatenate(mixed_parts, axis=1)

    weight_terms = lax.dot_general(
        grad_full, mixed, (((0,), (0,)), ((), ())), preferred_element_type=F32
    ).astype(BF16)
    weight = ring_gather(w_out, {2: halo[0], 3: (halo[1], before), 5: weight_terms})
    weight_part, early = ring_scatter(weight_terms)
    weight, _ = lax.optimization_barrier((weight, early))
    projection_sensitivity = weight_part.T * tokens_all ** (-0.5)
    grad_mixed = mm_nt(grad_full, weight).astype(BF16)

    back_parts = []
    for c in range(count):
        skip = c * part
        back_parts.append(
            pl.pallas_call(
                backward_kernel,
                grid=(part,),
                in_specs=[cols(tok, skip)] * 3
                + [cols(EDGE)] * 2
                + [cols(tok, skip)]
                + saved_specs,
                out_specs=[cols(tok)] * 3 + [cols(EDGE)] * 2 + [heads(DH, DH)],
                out_shape=[
                    shape((tok, part * DH), BF16),
                    shape((tok, part * DH), F32),
                    shape((tok, part * DH), F32),
                    shape((EDGE, part * DH), BF16),
                    shape((EDGE, part * DH), BF16),
                    shape((part, DH, DH), F32),
                ],
                scratch_shapes=[pltpu.VMEM((wide, DH), BF16)] * 2
                + [pltpu.VMEM((wide, DH), F32)] * 2,
                compiler_params=params,
                cost_estimate=cost(24 * part * tok * SPAN * DH, 40 * tok * part * DH),
                name="mixer_backward",
            )(queries, keys, values, *halo[c], grad_mixed, *kept[c])
        )
    dq = jnp.concatenate([p[0] for p in back_parts], axis=1)
    returned = [(shifted(p[3], -1), shifted(p[4], -1)) for p in back_parts]
    later = entering(jnp.concatenate([p[5] for p in back_parts], axis=0), True)
    mixed_late, _ = lax.optimization_barrier((mixed, back_parts[-1][5]))
    mixer_result = lax.psum_scatter(
        mm(mixed_late, weight).astype(BF16), "head", scatter_dimension=1, tiled=True
    )
    done = []
    for c in range(count):
        skip = c * part
        done.append(
            pl.pallas_call(
                finish_kernel,
                grid=(part,),
                in_specs=[cols(tok, skip)] * 2
                + [cols(tok)] * 2
                + [cols(EDGE)] * 2
                + [pl.BlockSpec((1, DH, DH), lambda h, skip=skip: (h + skip, 0, 0))],
                out_specs=[cols(tok)] * 2,
                out_shape=[shape((tok, part * DH), BF16)] * 2,
                compiler_params=params,
                cost_estimate=cost(4 * tok * part * DH * DH, 20 * tok * part * DH),
                name="mixer_finish",
            )(keys, values, back_parts[c][1], back_parts[c][2], *returned[c], later)
        )
    gk = jnp.concatenate([d[0] for d in done], axis=1)
    gv = jnp.concatenate([d[1] for d in done], axis=1)
    return (mixer_result, dq, gk, gv, projection_sensitivity)


def solution(mesh):
    placed = (
        P("seq", "head"),
        P("seq", "head"),
        P("seq", "head"),
        P("head", "seq"),
        P("seq", "head"),
    )
    return jax.shard_map(
        shards,
        mesh=mesh,
        in_specs=placed,
        out_specs=(
            P("seq", "head"),
            P("seq", "head"),
            P("seq", "head"),
            P("seq", "head"),
            P("head", "seq"),
        ),
        check_vma=False,
    )
```
